32 devices in a mesh: ep: 8 (over y, x, core), tp: 4 (over z).
Axes of the slice: x: 2, y: 2, z: 4, core: 2. Of those that a mesh axis runs over, the one named last changes fastest.
Arguments:
- query: bfloat16 [3, 256, 8192], P(None, 'ep', 'tp'), may hold values from -110 to 110
- step_key_value: bfloat16 [3, 2, 256, 512], P(None, None, 'ep', 'tp'), may hold values from -5 to 5
- key_value_cache: bfloat16 [2, 256, 128, 512], P(None, 'ep', None, 'tp'), may hold values from -5 to 5
- lengths: int32 [256], P('ep'), may hold values from 2 to 128, as said below
- hidden_in: bfloat16 [3, 256, 4096], P(None, ('ep', 'tp')), may hold values from -3 to 3
- norm_gain: float32 [4096], replicated, may hold values from 0.5 to 1.5
- w_out: bfloat16 [8192, 4096], P('tp', 'ep'), may hold values from -0.1875 to 0.1875
- routes: int32 [3, 256, 8], P(None, ('ep', 'tp')), may hold values from 0 to 31, all different within a row; in each aligned block of 8 rows (0 to 7, 8 to 15, ..., all dimensions but the last counted through in order) at most 8 rows name the same one
- gate_scores: float32 [3, 256, 8], P(None, ('ep', 'tp')), may hold values from 0.1 to 1
- expert_gate: bfloat16 [32, 4096, 768], P(('ep', 'tp')), may hold values from -0.09375 to 0.09375
- expert_up: bfloat16 [32, 4096, 768], P(('ep', 'tp')), may hold values from -0.09375 to 0.09375
- expert_down: bfloat16 [32, 768, 4096], P(('ep', 'tp')), may hold values from -0.21875 to 0.21875
Outputs:
- layer_out: bfloat16 [3, 256, 4096], P(None, ('ep', 'tp'))
The draws below stay inside these ranges and needn't reach their ends.
Inputs may be any that keep to these rules, and one draw needn't show every extreme that they name: `lengths`: every row has at least two filled cache positions, and some row fills all 128. `routes`: A row names 8 different experts. Within one step, the 8 rows of one device (aligned blocks of rows) name any one expert at most 8 times.
All inputs are finite; a program needn't handle non-finite values.
Results may differ from the reference program's by a relative error of at most 0.007.
Values may be sent and summed in bfloat16 or wider, within the bound.
A program may use at most 128 MiB of HBM per device.

```python
import math
import jax
import jax.numpy as jnp
import numpy as np
from jax import lax

D = 4096
QUERY_HEADS = 64
KEY_VALUE_HEADS = 4
HEAD_SIZE = 128
TOPK = 8
FFW = 768
DECODE_STEPS = 3
CACHE_POSITIONS = 128
ROW_OWN = 8
CAP = 8
TOTAL_ROWS = 256
EXPERTS = 32
N_EP = 8
N_TP = 4


def draw_key_value_cache(key, part):
    base_offset = jnp.clip(jax.random.normal(jax.random.fold_in(key, 11), (2, TOTAL_ROWS, CACHE_POSITIONS, KEY_VALUE_HEADS * HEAD_SIZE), jnp.float32), -5.0, 5.0)
    return base_offset.astype(jnp.bfloat16)


def draw_query(key, part):
    base_offset = jnp.clip(jax.random.normal(jax.random.fold_in(key, 13), (DECODE_STEPS, TOTAL_ROWS, QUERY_HEADS * HEAD_SIZE), jnp.float32), -5.0, 5.0)
    return base_offset.astype(jnp.bfloat16)


def draw_lengths(key, part):
    filled = jax.random.randint(jax.random.fold_in(key, 7), (TOTAL_ROWS,), 2, CACHE_POSITIONS + 1, jnp.int32)
    filled = filled.at[0].set(CACHE_POSITIONS)
    filled = filled.at[1].set(2)
    return filled


def shard_levels(rng, shape, shards, smallest, top_value):
    loudness = 1.0
    for position, blocks in shards:
        steps = jax.random.uniform(jax.random.fold_in(jax.random.fold_in(rng, 6), position), (blocks,), jnp.float32, smallest / len(shards), top_value / len(shards))
        loudness = loudness * jnp.repeat(jnp.exp(steps), shape[position] // blocks).reshape((-1,) + (1,) * (len(shape) - 1 - position))
    return loudness


def assign_block(rng, own, number, rows, number_of, top, limit, slope):
    order = jax.random.permutation(rng, number_of)
    packed, usual = portions_of(number_of, rows * top, limit, slope, True), portions_of(number_of, rows * top, limit, slope, False)
    places = jnp.arange(number_of)

    def named(tallies, rotation):
        used = int((tallies > 0).sum())
        fixed = max(1, used // 4)
        shifted = fixed + (places - fixed + rotation * (used - fixed)) % max(1, number_of - fixed)
        return jnp.zeros((number_of,), jnp.int32).at[order[jnp.where(places < fixed, places, shifted)]].set(jnp.asarray(tallies, jnp.int32))

    tallies = jnp.where(number % 4 == 0, named(packed, number // 4), named(usual, number - number // 4 - 1))
    mixed = jax.random.permutation(jax.random.fold_in(own, 3), number_of)
    source_of, receiver = mixed[0:number_of // 2 * 2:2], mixed[1:number_of // 2 * 2:2]
    room = jnp.minimum(tallies[source_of] - 1, limit - tallies[receiver]) // 2
    room = jnp.where((source_of == order[0]) | (receiver == order[0]) | (tallies[receiver] == 0), 0, jnp.maximum(room, 0))
    shifted = jax.random.randint(jax.random.fold_in(own, 4), (number_of // 2,), 0, 1 << 20) % (room + 1)
    tallies = tallies.at[source_of].add(-shifted).at[receiver].add(shifted)
    items = jnp.searchsorted(jnp.cumsum(tallies), jnp.arange(rows * top), side="right").astype(jnp.int32)
    listing = items.reshape(top, rows).T
    listing = listing[jax.random.permutation(jax.random.fold_in(own, 1), rows)]
    rotation = jax.random.randint(jax.random.fold_in(own, 2), (rows, 1), 0, top)
    return jnp.take_along_axis(listing, (jnp.arange(top)[None, :] + rotation) % top, axis=1)


def portions_of(amount, total, reach, slope, full):
    loads = [(1 << 20) // math.isqrt(grade ** slope) + 1 for grade in range(1, amount + 1)]
    largest = reach if full else min(reach, max(-(-total // amount), total * loads[0] // sum(loads)))
    least = 1 if total - largest >= amount - 1 else 0
    holding, surplus = [largest] + [least] * (amount - 1), total - largest - least * (amount - 1)
    while surplus > 0:
        movable = [i for i in range(1, amount) if holding[i] < largest] or [i for i in range(1, amount) if holding[i] < reach]
        mass, budget = sum([loads[i] for i in movable]), surplus
        for i in movable:
            addition = min(reach - holding[i], max(1, budget * loads[i] // mass), surplus)
            holding[i] = holding[i] + addition
            surplus = surplus - addition
    return np.array(holding)


def noise(stream_key, extent, width, reach, pieces=(), kind=jnp.bfloat16):
    result = width * jax.random.normal(stream_key, extent, jnp.float32)
    if pieces:
        result = result * shard_levels(stream_key, extent, pieces, -0.22, 0.18)
    return jnp.clip(result, -reach, reach).astype(kind)


def setup_inputs(seed: int = 0) -> dict:
    key_list = jax.random.split(jax.random.key(seed), 13)
    query = draw_query(jax.random.fold_in(key_list[12], 71), 0)
    step_key_value = noise(key_list[1], (DECODE_STEPS, 2, TOTAL_ROWS, KEY_VALUE_HEADS * HEAD_SIZE), 1.0, 5.0, ((2, 8), (3, 4)))
    key_value_cache = draw_key_value_cache(jax.random.fold_in(key_list[12], 71), 0)
    lengths = draw_lengths(jax.random.fold_in(key_list[12], 71), 0)
    hidden_in = noise(key_list[4], (DECODE_STEPS, TOTAL_ROWS, D), 0.5, 3.0, ((1, 32),))
    norm_gain = jnp.clip(1.0 + 0.1 * jax.random.normal(key_list[5], (D,), jnp.float32), 0.5, 1.5)
    w_out = noise(key_list[6], (QUERY_HEADS * HEAD_SIZE, D), (QUERY_HEADS * HEAD_SIZE // 8) ** -0.5, 0.1875, ((0, 4), (1, 8)))
    routes_keys = jax.random.split(jax.random.fold_in(key_list[7], 1), DECODE_STEPS * TOTAL_ROWS // ROW_OWN)
    routes_turns = jax.random.permutation(jax.random.fold_in(key_list[7], 3), DECODE_STEPS * TOTAL_ROWS // ROW_OWN)
    routes = jax.vmap(lambda own, number: assign_block(jax.random.fold_in(key_list[7], 2), own, number, ROW_OWN, EXPERTS, TOPK, CAP, 2))(routes_keys, routes_turns).reshape((DECODE_STEPS, TOTAL_ROWS, TOPK))
    gate_scores = jnp.clip(0.1 + 0.9 * jax.random.uniform(key_list[8], (DECODE_STEPS, TOTAL_ROWS, TOPK), jnp.float32) ** shard_levels(key_list[8], (DECODE_STEPS, TOTAL_ROWS, TOPK), ((1, 32),), -0.2, 0.2), 0.1, 1.0)
    expert_gate = noise(key_list[9], (EXPERTS, D, FFW), D ** -0.5, 0.09375, ((0, 32),))
    expert_up = noise(key_list[10], (EXPERTS, D, FFW), D ** -0.5, 0.09375, ((0, 32),))
    expert_down = noise(key_list[11], (EXPERTS, FFW, D), FFW ** -0.5, 0.21875, ((0, 32),))
    return dict(query=query, step_key_value=step_key_value, key_value_cache=key_value_cache, lengths=lengths, hidden_in=hidden_in, norm_gain=norm_gain, w_out=w_out, routes=routes, gate_scores=gate_scores, expert_gate=expert_gate, expert_up=expert_up, expert_down=expert_down)


masked_score = -1e+30
norm_eps = 1e-06

def mix_experts(normed, route_ids, weights, expert_gate, expert_up, expert_down):
    flat_ids = route_ids.reshape(-1)
    flat_weights = weights.reshape(-1)
    most_rows = N_EP * N_TP * CAP
    block_rows = min(64, most_rows)

    def per_expert(total, inputs):
        expert, gate_weights, up_weights, down_weights = inputs
        matches = flat_ids == expert
        count = jnp.sum(matches.astype(jnp.int32))
        order = jnp.nonzero(matches, size=most_rows, fill_value=0)[0].astype(jnp.int32)

        def one_block(index, running):
            picked = lax.dynamic_slice_in_dim(order, (index * block_rows).astype(jnp.int32), block_rows)
            live = index * block_rows + jnp.arange(block_rows, dtype=jnp.int32) < count
            row_ids = picked // TOPK
            inputs_rows = normed[row_ids]
            gate_act = jnp.dot(inputs_rows, gate_weights, preferred_element_type=jnp.float32)
            up_act = jnp.dot(inputs_rows, up_weights, preferred_element_type=jnp.float32)
            hidden = (jax.nn.silu(gate_act) * up_act).astype(jnp.bfloat16)
            expert_out = jnp.dot(hidden, down_weights, preferred_element_type=jnp.float32).astype(jnp.bfloat16)
            scaled = jnp.where(live, flat_weights[picked], jnp.zeros_like(flat_weights[picked]))
            return running.at[row_ids].add(scaled[:, None] * expert_out.astype(jnp.float32))
        blocks = (count + block_rows - 1) // block_rows
        total = lax.fori_loop(jnp.int32(0), blocks.astype(jnp.int32), one_block, total)
        return (total, None)
    start = jnp.zeros((normed.shape[0], D), jnp.float32)
    experts_list = jnp.arange(EXPERTS, dtype=jnp.int32)
    total, _ = lax.scan(per_expert, start, (experts_list, expert_gate, expert_up, expert_down))
    return total

def reference(query, step_key_value, key_value_cache, lengths, hidden_in, norm_gain, w_out, routes, gate_scores, expert_gate, expert_up, expert_down):
    query_group = QUERY_HEADS // KEY_VALUE_HEADS
    score_scale = HEAD_SIZE ** (-0.5)
    stored_keys = key_value_cache[0].astype(jnp.float32).reshape(TOTAL_ROWS, CACHE_POSITIONS, KEY_VALUE_HEADS, HEAD_SIZE)
    stored_values = key_value_cache[1].astype(jnp.float32).reshape(TOTAL_ROWS, CACHE_POSITIONS, KEY_VALUE_HEADS, HEAD_SIZE)
    usable = jnp.arange(CACHE_POSITIONS, dtype=jnp.int32)[None, :] < lengths[:, None]
    results = []
    for decode_step in range(DECODE_STEPS):
        query_rows = query[decode_step].astype(jnp.float32).reshape(TOTAL_ROWS, KEY_VALUE_HEADS, query_group, HEAD_SIZE)
        incoming_keys = step_key_value[:decode_step + 1, 0].astype(jnp.float32).reshape(decode_step + 1, TOTAL_ROWS, KEY_VALUE_HEADS, HEAD_SIZE)
        incoming_values = step_key_value[:decode_step + 1, 1].astype(jnp.float32).reshape(decode_step + 1, TOTAL_ROWS, KEY_VALUE_HEADS, HEAD_SIZE)
        cache_scores = jnp.einsum('rgqd,rjgd->rgqj', query_rows, stored_keys) * score_scale
        cache_scores = jnp.where(usable[:, None, None, :], cache_scores, masked_score)
        fresh_scores = jnp.einsum('rgqd,jrgd->rgqj', query_rows, incoming_keys) * score_scale
        scores = jnp.concatenate([cache_scores, fresh_scores], axis=-1)
        top = lax.optimization_barrier(jnp.max(scores, axis=-1, keepdims=True))
        raised = jnp.exp(scores - top)
        probs = (raised / lax.optimization_barrier(jnp.sum(raised, axis=-1, keepdims=True))).astype(jnp.bfloat16)
        probs_wide = probs.astype(jnp.float32)
        attended = jnp.einsum('rgqj,rjgd->rgqd', probs_wide[..., :CACHE_POSITIONS], stored_values)
        attended = attended + jnp.einsum('rgqj,jrgd->rgqd', probs_wide[..., CACHE_POSITIONS:], incoming_values)
        attended = attended.astype(jnp.bfloat16).reshape(TOTAL_ROWS, QUERY_HEADS * HEAD_SIZE)
        projected = jnp.dot(attended, w_out, preferred_element_type=jnp.float32).astype(jnp.bfloat16)
        residual = hidden_in[decode_step].astype(jnp.float32) + projected.astype(jnp.float32)
        mean_square = lax.optimization_barrier(jnp.mean(residual * residual, axis=-1, keepdims=True))
        normed = (residual * lax.rsqrt(mean_square + norm_eps) * norm_gain).astype(jnp.bfloat16)
        weights = gate_scores[decode_step] / lax.optimization_barrier(jnp.sum(gate_scores[decode_step], axis=-1, keepdims=True))
        expert_mix = mix_experts(normed, routes[decode_step], weights, expert_gate, expert_up, expert_down)
        results.append((residual + expert_mix).astype(jnp.bfloat16))
    return jnp.stack(results)
```

```python
import jax
import jax.numpy as jnp
from jax import lax
from jax.sharding import PartitionSpec as P

HEAD_SIZE = 128
GROUPS = ((0, 1, 2),)

masked_score = -1e30
norm_eps = 1e-06


def attend(query, step_key_value, key_value_cache, lengths):
    steps, row_dev, columns = query.shape
    heads_dev = columns // HEAD_SIZE
    cache_len = key_value_cache.shape[2]
    score_scale = HEAD_SIZE ** (-0.5)
    rows = query.reshape(steps, row_dev, heads_dev, HEAD_SIZE).transpose(1, 0, 2, 3)
    rows = rows.reshape(row_dev, steps * heads_dev, HEAD_SIZE)
    fresh = step_key_value.transpose(1, 2, 0, 3)
    usable = jnp.arange(cache_len, dtype=jnp.int32)[None, :] < lengths[:, None]
    cache_scores = (
        jnp.einsum("rhd,rjd->rhj", rows, key_value_cache[0], preferred_element_type=jnp.float32)
        * score_scale
    )
    cache_scores = jnp.where(usable[:, None, :], cache_scores, masked_score)
    fresh_scores = (
        jnp.einsum("rhd,rjd->rhj", rows, fresh[0], preferred_element_type=jnp.float32)
        * score_scale
    )
    step_of = jnp.arange(steps * heads_dev, dtype=jnp.int32) // heads_dev
    known = jnp.arange(steps, dtype=jnp.int32)[None, :] <= step_of[:, None]
    fresh_scores = jnp.where(known[None], fresh_scores, masked_score)
    top = jnp.maximum(
        jnp.max(cache_scores, axis=-1, keepdims=True), jnp.max(fresh_scores, axis=-1, keepdims=True)
    )
    cache_raised = jnp.exp(cache_scores - top)
    fresh_raised = jnp.exp(fresh_scores - top)
    total = jnp.sum(cache_raised, axis=-1, keepdims=True) + jnp.sum(
        fresh_raised, axis=-1, keepdims=True
    )
    cache_probs = (cache_raised / total).astype(jnp.bfloat16)
    fresh_probs = (fresh_raised / total).astype(jnp.bfloat16)
    attended = jnp.einsum(
        "rhj,rjd->rhd", cache_probs, key_value_cache[1], preferred_element_type=jnp.float32
    ) + jnp.einsum("rhj,rjd->rhd", fresh_probs, fresh[1], preferred_element_type=jnp.float32)
    attended = attended.astype(jnp.bfloat16).reshape(row_dev, steps, heads_dev * HEAD_SIZE)
    return attended.transpose(1, 0, 2)


def per_device(
    query,
    step_key_value,
    key_value_cache,
    lengths,
    hidden_in,
    norm_gain,
    w_out,
    routes,
    gate_scores,
    expert_gate,
    expert_up,
    expert_down,
):
    ep_count = lax.axis_size("ep")
    tp_count = lax.axis_size("tp")
    row_own = hidden_in.shape[1]
    width = hidden_in.shape[2]
    cols = w_out.shape[1]
    expert_count = ep_count * tp_count * expert_gate.shape[0]
    mine = lax.axis_index("ep") * tp_count + lax.axis_index("tp")

    weights = gate_scores / jnp.sum(gate_scores, axis=-1, keepdims=True)
    named = routes[..., None] == jnp.arange(expert_count, dtype=jnp.int32)
    dense = jnp.sum(jnp.where(named, weights[..., None], 0.0), axis=2)

    attended = attend(query, step_key_value, key_value_cache, lengths)
    results = []
    for group in GROUPS:
        first, count = group[0], len(group)
        group_dense = dense[first : first + count].reshape(count * row_own, expert_count)
        all_dense = lax.all_gather(group_dense, ("ep", "tp"), axis=0, tiled=True)
        my_weight = lax.dynamic_slice_in_dim(all_dense, mine, 1, axis=1)

        part = attended[first : first + count]
        row_dev = part.shape[1]
        everyone = lax.all_gather(part.reshape(count * row_dev, -1), "ep", axis=0, tiled=True)
        partial_sums = jnp.dot(everyone, w_out, preferred_element_type=jnp.float32)
        grouped = partial_sums.reshape(ep_count, count, tp_count, row_own, cols)
        grouped = grouped.transpose(2, 0, 1, 3, 4).reshape(tp_count * ep_count * count * row_own, cols)
        summed = lax.psum_scatter(grouped, "tp", scatter_dimension=0, tiled=True)
        projected = summed.reshape(ep_count, count * row_own, cols).astype(jnp.bfloat16)
        row_major = lax.all_to_all(
            projected, "ep", split_axis=0, concat_axis=2, tiled=True
        ).reshape(count * row_own, width)
        own = hidden_in[first : first + count].reshape(count * row_own, width)
        residual = own.astype(jnp.float32) + row_major.astype(jnp.float32)
        mean_square = jnp.mean(residual * residual, axis=-1, keepdims=True)
        normed = (residual * lax.rsqrt(mean_square + norm_eps) * norm_gain).astype(jnp.bfloat16)

        flat_rows = lax.all_gather(normed, ("ep", "tp"), axis=0, tiled=True)
        gate_act = jnp.dot(flat_rows, expert_gate[0], preferred_element_type=jnp.float32)
        up_act = jnp.dot(flat_rows, expert_up[0], preferred_element_type=jnp.float32)
        hidden = (jax.nn.silu(gate_act) * up_act).astype(jnp.bfloat16)
        expert_out = jnp.dot(hidden, expert_down[0], preferred_element_type=jnp.float32).astype(
            jnp.bfloat16
        )
        share = (expert_out.astype(jnp.float32) * my_weight).astype(jnp.bfloat16)
        mix = lax.psum_scatter(share, ("ep", "tp"), scatter_dimension=0, tiled=True)
        layer_out = (residual + mix.astype(jnp.float32)).astype(jnp.bfloat16)
        results.append(layer_out.reshape(count, row_own, width))
    return jnp.concatenate(results) if len(results) > 1 else results[0]


def solution(mesh):
    placed = (
        P(None, "ep", "tp"),
        P(None, None, "ep", "tp"),
        P(None, "ep", None, "tp"),
        P("ep"),
        P(None, ("ep", "tp"), None),
        P(),
        P("tp", "ep"),
        P(None, ("ep", "tp"), None),
        P(None, ("ep", "tp"), None),
        P(("ep", "tp"), None, None),
        P(("ep", "tp"), None, None),
        P(("ep", "tp"), None, None),
    )
    return jax.shard_map(
        per_device,
        mesh=mesh,
        in_specs=placed,
        out_specs=P(None, ("ep", "tp"), None),
        check_vma=False,
    )
```

```python
import functools

import jax
import jax.numpy as jnp
from jax import lax
from jax.experimental import pallas as pl
from jax.experimental.pallas import tpu as pltpu
from jax.sharding import PartitionSpec as P

HEAD_SIZE = 128
CHUNKS = 4
MESH = pl.DeviceIdType.MESH

masked_score = -1e30
norm_eps = 1e-06


def greet(devices):
    barrier = pltpu.get_barrier_semaphore()
    for device in devices:
        pl.semaphore_signal(barrier, inc=1, device_id=device, device_id_type=MESH)
    pl.semaphore_wait(barrier, len(devices))


def gather_kernel(chips, depth, x_ref, out_ref, own_sem, z_send, z_recv, c_send, c_recv, p_send, p_recv):
    ep, tp = lax.axis_index("ep"), lax.axis_index("tp")
    chip, core = ep // 2, ep % 2
    partner = (chip * 2 + 1 - core, tp)
    chip_of = [(chip + j) % chips for j in range(chips)]
    chip_from = [(chip + chips - j) % chips for j in range(chips)]
    if depth > 1:
        tp_of = [(tp + t) % depth for t in range(depth)]
        tp_from = [(tp + depth - t) % depth for t in range(depth)]
    else:
        tp_from = [0]
    greet(
        [partner]
        + [(chip_of[j] * 2 + core, tp) for j in range(1, chips)]
        + [(ep, tp_of[t]) for t in range(1, depth)]
    )

    def push(src, slot, send, recv, device):
        copy = pltpu.make_async_remote_copy(
            src_ref=src,
            dst_ref=out_ref.at[slot],
            send_sem=send,
            recv_sem=recv,
            device_id=device,
            device_id_type=MESH,
        )
        copy.start()
        return copy

    def arrival(slot, recv):
        pltpu.make_async_remote_copy(
            src_ref=out_ref.at[slot],
            dst_ref=out_ref.at[slot],
            send_sem=recv,
            recv_sem=recv,
            device_id=partner,
            device_id_type=MESH,
        ).wait_recv()

    sent = []
    own_slot = (chip, core, tp_from[0])
    for t in range(1, depth):
        sent.append(push(x_ref, own_slot, z_send.at[t], z_recv.at[t], (ep, tp_of[t])))
    own = pltpu.make_async_copy(x_ref, out_ref.at[own_slot], own_sem)
    own.start()
    for t in range(depth):
        slot = (chip, core, tp_from[t])
        src = x_ref
        if t > 0:
            arrival(slot, z_recv.at[t])
            src = out_ref.at[slot]
        for j in range(chips - 1, 0, -1):
            device = (chip_of[j] * 2 + core, tp)
            sent.append(push(src, slot, c_send.at[t, j], c_recv.at[t, j], device))
        sent.append(push(src, slot, p_send.at[t, 0], p_recv.at[t, 0], partner))
    for t in range(depth):
        for j in range(1, chips):
            slot = (chip_from[j], core, tp_from[t])
            arrival(slot, c_recv.at[t, j])
            sent.append(push(out_ref.at[slot], slot, p_send.at[t, j], p_recv.at[t, j], partner))
    for t in range(depth):
        for j in range(chips):
            arrival((chip_from[j], 1 - core, tp_from[t]), p_recv.at[t, j])
    own.wait()
    for copy in sent:
        copy.wait_send()


def gather(x, chips, depth, collective_id):
    rows, columns = x.shape
    dma = pltpu.SemaphoreType.DMA
    return pl.pallas_call(
        functools.partial(gather_kernel, chips, depth),
        out_shape=jax.ShapeDtypeStruct((chips, 2, depth, rows, columns), x.dtype),
        in_specs=[pl.BlockSpec(memory_space=pl.ANY)],
        out_specs=pl.BlockSpec(memory_space=pl.ANY),
        scratch_shapes=[
            dma,
            dma((depth,)),
            dma((depth,)),
            dma((depth, chips)),
            dma((depth, chips)),
            dma((depth, chips)),
            dma((depth, chips)),
        ],
        compiler_params=pltpu.CompilerParams(collective_id=collective_id, has_side_effects=True),
    )(x).reshape(chips * 2 * depth * rows, columns)


def scatter_kernel(
    chips,
    depth,
    share_ref,
    residual_ref,
    out_ref,
    own,
    from_core,
    from_chips,
    mid,
    from_z,
    kept,
    own_sem,
    p_send,
    p_recv,
    c_send,
    c_recv,
    z_send,
    z_recv,
):
    ep, tp = lax.axis_index("ep"), lax.axis_index("tp")
    chip, core = ep // 2, ep % 2
    partner = (chip * 2 + 1 - core, tp)
    chip_of = [(chip + j) % chips for j in range(chips)]
    tp_of = [(tp + t) % depth for t in range(depth)]
    peers = [(chip_of[j] * 2 + core, tp) for j in range(chips)]
    layers = [(ep, tp_of[t]) for t in range(depth)]
    greet([partner] + peers[1:] + layers[1:])
    part = own.shape[-1]
    order = list(range(chips - 1, -1, -1))

    def columns(k):
        return pl.ds(k * part, part)

    def to_core(k, j):
        return pltpu.make_async_remote_copy(
            src_ref=share_ref.at[chip_of[j], 1 - core, :, :, columns(k)],
            dst_ref=from_core.at[k, j],
            send_sem=p_send.at[k, j],
            recv_sem=p_recv.at[k, j],
            device_id=partner,
            device_id_type=MESH,
        )

    def load(k, j):
        return pltpu.make_async_copy(
            share_ref.at[chip_of[j], core, :, :, columns(k)], own.at[k, j], own_sem.at[k, j]
        )

    def to_chip(k, j):
        return pltpu.make_async_remote_copy(
            src_ref=own.at[k, j],
            dst_ref=from_chips.at[k, j],
            send_sem=c_send.at[k, j],
            recv_sem=c_recv.at[k, j],
            device_id=peers[j],
            device_id_type=MESH,
        )

    def to_layer(k, t):
        return pltpu.make_async_remote_copy(
            src_ref=mid.at[k, t],
            dst_ref=from_z.at[k, t],
            send_sem=z_send.at[k, t],
            recv_sem=z_recv.at[k, t],
            device_id=layers[t],
            device_id_type=MESH,
        )

    def over_chips(k):
        for j in range(1, chips):
            to_chip(k, j).wait_recv()
        for t in list(range(1, depth)) + [0]:
            total = own[k, 0, tp_of[t]].astype(jnp.float32)
            for j in range(1, chips):
                total += from_chips[k, j, tp_of[t]].astype(jnp.float32)
            if t > 0:
                mid[k, t] = total.astype(mid.dtype)
                to_layer(k, t).start()
            else:
                kept[k] = total

    def finish(k):
        total = kept[k] + residual_ref[:, columns(k)]
        for t in range(1, depth):
            to_layer(k, t).wait_recv()
            total += from_z[k, t].astype(jnp.float32)
        out_ref[:, columns(k)] = total.astype(out_ref.dtype)

    for k in range(CHUNKS):
        for j in order:
            to_core(k, j).start()
            load(k, j).start()
    for k in range(CHUNKS):
        for j in order:
            to_core(k, j).wait_recv()
            load(k, j).wait()
            for t in range(depth):
                own[k, j, t] = (
                    own[k, j, t].astype(jnp.float32) + from_core[k, j, t].astype(jnp.float32)
                ).astype(own.dtype)
            if j > 0:
                to_chip(k, j).start()
        if k > 0:
            over_chips(k - 1)
    over_chips(CHUNKS - 1)
    for k in range(CHUNKS):
        finish(k)
    for k in range(CHUNKS):
        for j in range(chips):
            to_core(k, j).wait_send()
            if j > 0:
                to_chip(k, j).wait_send()
        for t in range(1, depth):
            to_layer(k, t).wait_send()


def scatter(share, residual, chips, depth, collective_id):
    rows, width = residual.shape
    part = width // CHUNKS
    dma = pltpu.SemaphoreType.DMA
    vmem = pltpu.VMEM
    blocks = (CHUNKS, chips, depth, rows, part)
    return pl.pallas_call(
        functools.partial(scatter_kernel, chips, depth),
        out_shape=jax.ShapeDtypeStruct((rows, width), jnp.bfloat16),
        in_specs=[
            pl.BlockSpec(memory_space=pl.ANY),
            pl.BlockSpec(memory_space=pltpu.VMEM),
        ],
        out_specs=pl.BlockSpec(memory_space=pltpu.VMEM),
        scratch_shapes=[
            vmem(blocks, jnp.bfloat16),
            vmem(blocks, jnp.bfloat16),
            vmem(blocks, jnp.bfloat16),
            vmem((CHUNKS, depth, rows, part), jnp.bfloat16),
            vmem((CHUNKS, depth, rows, part), jnp.bfloat16),
            vmem((CHUNKS, rows, part), jnp.float32),
            dma((CHUNKS, chips)),
            dma((CHUNKS, chips)),
            dma((CHUNKS, chips)),
            dma((CHUNKS, chips)),
            dma((CHUNKS, chips)),
            dma((CHUNKS, depth)),
            dma((CHUNKS, depth)),
        ],
        compiler_params=pltpu.CompilerParams(
            collective_id=collective_id, has_side_effects=True, vmem_limit_bytes=56 * 1024 * 1024
        ),
    )(share.reshape(chips, 2, depth, rows, width), residual)


def attend(query, step_key_value, key_value_cache, lengths, owners):
    steps, row_dev, columns = query.shape
    heads_dev = columns // HEAD_SIZE
    cache_len = key_value_cache.shape[2]
    score_scale = HEAD_SIZE ** (-0.5)
    rows = query.reshape(steps, row_dev, heads_dev, HEAD_SIZE).transpose(1, 0, 2, 3)
    rows = rows.reshape(row_dev, steps * heads_dev, HEAD_SIZE)
    fresh = step_key_value.transpose(1, 2, 0, 3)
    usable = jnp.arange(cache_len, dtype=jnp.int32)[None, :] < lengths[:, None]
    cache_scores = (
        jnp.einsum("rhd,rjd->rhj", rows, key_value_cache[0], preferred_element_type=jnp.float32)
        * score_scale
    )
    cache_scores = jnp.where(usable[:, None, :], cache_scores, masked_score)
    fresh_scores = (
        jnp.einsum("rhd,rjd->rhj", rows, fresh[0], preferred_element_type=jnp.float32)
        * score_scale
    )
    step_of = jnp.arange(steps * heads_dev, dtype=jnp.int32) // heads_dev
    known = jnp.arange(steps, dtype=jnp.int32)[None, :] <= step_of[:, None]
    fresh_scores = jnp.where(known[None], fresh_scores, masked_score)
    top = jnp.maximum(
        jnp.max(cache_scores, axis=-1, keepdims=True), jnp.max(fresh_scores, axis=-1, keepdims=True)
    )
    cache_raised = jnp.exp(cache_scores - top)
    fresh_raised = jnp.exp(fresh_scores - top)
    total = jnp.sum(cache_raised, axis=-1, keepdims=True) + jnp.sum(
        fresh_raised, axis=-1, keepdims=True
    )
    cache_probs = (cache_raised / total).astype(jnp.bfloat16)
    fresh_probs = (fresh_raised / total).astype(jnp.bfloat16)
    attended = jnp.einsum(
        "rhj,rjd->rhd", cache_probs, key_value_cache[1], preferred_element_type=jnp.float32
    ) + jnp.einsum("rhj,rjd->rhd", fresh_probs, fresh[1], preferred_element_type=jnp.float32)
    attended = attended.astype(jnp.bfloat16).reshape(owners, row_dev // owners, steps, columns)
    return attended.transpose(0, 2, 1, 3).reshape(steps * row_dev, columns)


def per_device(
    query,
    step_key_value,
    key_value_cache,
    lengths,
    hidden_in,
    norm_gain,
    w_out,
    routes,
    gate_scores,
    expert_gate,
    expert_up,
    expert_down,
):
    ep_count = lax.axis_size("ep")
    tp_count = lax.axis_size("tp")
    chips = ep_count // 2
    steps, row_own = hidden_in.shape[:2]
    width = hidden_in.shape[2]
    cols = w_out.shape[1]
    expert_count = ep_count * tp_count * expert_gate.shape[0]
    mine = lax.axis_index("ep") * tp_count + lax.axis_index("tp")

    weights = gate_scores / jnp.sum(gate_scores, axis=-1, keepdims=True)
    named = routes[..., None] == jnp.arange(expert_count, dtype=jnp.int32)
    dense = jnp.sum(jnp.where(named, weights[..., None], 0.0), axis=2)

    all_dense = lax.all_gather(
        dense.reshape(steps * row_own, expert_count), ("ep", "tp"), axis=0, tiled=True
    )
    my_weight = lax.dynamic_slice_in_dim(all_dense, mine, 1, axis=1)

    attended = attend(query, step_key_value, key_value_cache, lengths, tp_count)
    everyone = gather(attended, chips, 1, 1)
    partial_sums = jnp.dot(everyone, w_out, preferred_element_type=jnp.float32)
    partial_sums = partial_sums.astype(jnp.bfloat16).reshape(-1, steps * row_own, cols)
    arrived = lax.all_to_all(partial_sums, ("ep", "tp"), split_axis=0, concat_axis=0, tiled=True)
    arrived = arrived.reshape(ep_count, tp_count, steps * row_own, cols)
    projected = jnp.sum(arrived.astype(jnp.float32), axis=1).astype(jnp.bfloat16)
    row_major = projected.transpose(1, 0, 2).reshape(steps * row_own, width)
    own = hidden_in.reshape(steps * row_own, width)
    residual = own.astype(jnp.float32) + row_major.astype(jnp.float32)
    mean_square = jnp.mean(residual * residual, axis=-1, keepdims=True)
    normed = (residual * lax.rsqrt(mean_square + norm_eps) * norm_gain).astype(jnp.bfloat16)

    flat_rows = gather(normed, chips, tp_count, 2)
    gate_act = jnp.dot(flat_rows, expert_gate[0], preferred_element_type=jnp.float32)
    up_act = jnp.dot(flat_rows, expert_up[0], preferred_element_type=jnp.float32)
    hidden = (jax.nn.silu(gate_act) * up_act).astype(jnp.bfloat16)
    expert_out = jnp.dot(hidden, expert_down[0], preferred_element_type=jnp.float32).astype(
        jnp.bfloat16
    )
    share = (expert_out.astype(jnp.float32) * my_weight).astype(jnp.bfloat16)
    layer_out = scatter(share, residual, chips, tp_count, 3)
    return layer_out.reshape(steps, row_own, width)


def solution(mesh):
    placed = (
        P(None, "ep", "tp"),
        P(None, None, "ep", "tp"),
        P(None, "ep", None, "tp"),
        P("ep"),
        P(None, ("ep", "tp"), None),
        P(),
        P("tp", "ep"),
        P(None, ("ep", "tp"), None),
        P(None, ("ep", "tp"), None),
        P(("ep", "tp"), None, None),
        P(("ep", "tp"), None, None),
        P(("ep", "tp"), None, None),
    )
    return jax.shard_map(
        per_device,
        mesh=mesh,
        in_specs=placed,
        out_specs=P(None, ("ep", "tp"), None),
        check_vma=False,
    )
```

```python
import functools

import jax
import jax.numpy as jnp
from jax import lax
from jax.experimental import pallas as pl
from jax.experimental.pallas import tpu as pltpu
from jax.sharding import PartitionSpec as P

HEAD_SIZE = 128
CHUNKS = 4
MESH = pl.DeviceIdType.MESH

masked_score = -1e30
norm_eps = 1e-06


def greet(devices):
    barrier = pltpu.get_barrier_semaphore()
    for device in devices:
        pl.semaphore_signal(barrier, inc=1, device_id=device, device_id_type=MESH)
    pl.semaphore_wait(barrier, len(devices))


def gather_kernel(chips, depth, x_ref, out_ref, own_sem, z_send, z_recv, c_send, c_recv, p_send, p_recv):
    ep, tp = lax.axis_index("ep"), lax.axis_index("tp")
    chip, core = ep // 2, ep % 2
    partner = (chip * 2 + 1 - core, tp)
    chip_of = [(chip + j) % chips for j in range(chips)]
    chip_from = [(chip + chips - j) % chips for j in range(chips)]
    if depth > 1:
        tp_of = [(tp + t) % depth for t in range(depth)]
        tp_from = [(tp + depth - t) % depth for t in range(depth)]
    else:
        tp_from = [0]
    greet(
        [partner]
        + [(chip_of[j] * 2 + core, tp) for j in range(1, chips)]
        + [(ep, tp_of[t]) for t in range(1, depth)]
    )

    def push(src, slot, send, recv, device):
        copy = pltpu.make_async_remote_copy(
            src_ref=src,
            dst_ref=out_ref.at[slot],
            send_sem=send,
            recv_sem=recv,
            device_id=device,
            device_id_type=MESH,
        )
        copy.start()
        return copy

    def arrival(slot, recv):
        pltpu.make_async_remote_copy(
            src_ref=out_ref.at[slot],
            dst_ref=out_ref.at[slot],
            send_sem=recv,
            recv_sem=recv,
            device_id=partner,
            device_id_type=MESH,
        ).wait_recv()

    sent = []
    own_slot = (chip, core, tp_from[0])
    for t in range(1, depth):
        sent.append(push(x_ref, own_slot, z_send.at[t], z_recv.at[t], (ep, tp_of[t])))
    own = pltpu.make_async_copy(x_ref, out_ref.at[own_slot], own_sem)
    own.start()
    for t in range(depth):
        slot = (chip, core, tp_from[t])
        src = x_ref
        if t > 0:
            arrival(slot, z_recv.at[t])
            src = out_ref.at[slot]
        for j in range(chips - 1, 0, -1):
            device = (chip_of[j] * 2 + core, tp)
            sent.append(push(src, slot, c_send.at[t, j], c_recv.at[t, j], device))
        sent.append(push(src, slot, p_send.at[t, 0], p_recv.at[t, 0], partner))
    for t in range(depth):
        for j in range(1, chips):
            slot = (chip_from[j], core, tp_from[t])
            arrival(slot, c_recv.at[t, j])
            sent.append(push(out_ref.at[slot], slot, p_send.at[t, j], p_recv.at[t, j], partner))
    for t in range(depth):
        for j in range(chips):
            arrival((chip_from[j], 1 - core, tp_from[t]), p_recv.at[t, j])
    own.wait()
    for copy in sent:
        copy.wait_send()


def gather(x, chips, depth, collective_id):
    rows, columns = x.shape
    dma = pltpu.SemaphoreType.DMA
    return pl.pallas_call(
        functools.partial(gather_kernel, chips, depth),
        out_shape=jax.ShapeDtypeStruct((chips, 2, depth, rows, columns), x.dtype),
        in_specs=[pl.BlockSpec(memory_space=pl.ANY)],
        out_specs=pl.BlockSpec(memory_space=pl.ANY),
        scratch_shapes=[
            dma,
            dma((depth,)),
            dma((depth,)),
            dma((depth, chips)),
            dma((depth, chips)),
            dma((depth, chips)),
            dma((depth, chips)),
        ],
        compiler_params=pltpu.CompilerParams(collective_id=collective_id, has_side_effects=True),
    )(x).reshape(chips * 2 * depth * rows, columns)


def scatter_kernel(
    chips,
    depth,
    share_ref,
    residual_ref,
    out_ref,
    own,
    from_core,
    from_chips,
    mid,
    from_z,
    kept,
    own_sem,
    p_send,
    p_recv,
    c_send,
    c_recv,
    z_send,
    z_recv,
):
    ep, tp = lax.axis_index("ep"), lax.axis_index("tp")
    chip, core = ep // 2, ep % 2
    partner = (chip * 2 + 1 - core, tp)
    chip_of = [(chip + j) % chips for j in range(chips)]
    tp_of = [(tp + t) % depth for t in range(depth)]
    peers = [(chip_of[j] * 2 + core, tp) for j in range(chips)]
    layers = [(ep, tp_of[t]) for t in range(depth)]
    greet([partner] + peers[1:] + layers[1:])
    part = own.shape[-1]
    order = list(range(chips - 1, -1, -1))

    def columns(k):
        return pl.ds(k * part, part)

    def to_core(k, j):
        return pltpu.make_async_remote_copy(
            src_ref=share_ref.at[chip_of[j], 1 - core, :, :, columns(k)],
            dst_ref=from_core.at[k, j],
            send_sem=p_send.at[k, j],
            recv_sem=p_recv.at[k, j],
            device_id=partner,
            device_id_type=MESH,
        )

    def load(k, j):
        return pltpu.make_async_copy(
            share_ref.at[chip_of[j], core, :, :, columns(k)], own.at[k, j], own_sem.at[k, j]
        )

    def to_chip(k, j):
        return pltpu.make_async_remote_copy(
            src_ref=own.at[k, j],
            dst_ref=from_chips.at[k, j],
            send_sem=c_send.at[k, j],
            recv_sem=c_recv.at[k, j],
            device_id=peers[j],
            device_id_type=MESH,
        )

    def to_layer(k, t):
        return pltpu.make_async_remote_copy(
            src_ref=mid.at[k, t],
            dst_ref=from_z.at[k, t],
            send_sem=z_send.at[k, t],
            recv_sem=z_recv.at[k, t],
            device_id=layers[t],
            device_id_type=MESH,
        )

    def over_chips(k):
        for j in range(1, chips):
            to_chip(k, j).wait_recv()
        for t in list(range(1, depth)) + [0]:
            total = own[k, 0, tp_of[t]].astype(jnp.float32)
            for j in range(1, chips):
                total += from_chips[k, j, tp_of[t]].astype(jnp.float32)
            if t > 0:
                mid[k, t] = total.astype(mid.dtype)
                to_layer(k, t).start()
            else:
                kept[k] = total

    def finish(k):
        total = kept[k] + residual_ref[:, columns(k)]
        for t in range(1, depth):
            to_layer(k, t).wait_recv()
            total += from_z[k, t].astype(jnp.float32)
        out_ref[:, columns(k)] = total.astype(out_ref.dtype)

    for k in range(CHUNKS):
        for j in order:
            to_core(k, j).start()
            load(k, j).start()
    for k in range(CHUNKS):
        for j in order:
            to_core(k, j).wait_recv()
            load(k, j).wait()
            for t in range(depth):
                own[k, j, t] = (
                    own[k, j, t].astype(jnp.float32) + from_core[k, j, t].astype(jnp.float32)
                ).astype(own.dtype)
            if j > 0:
                to_chip(k, j).start()
        if k > 0:
            over_chips(k - 1)
    over_chips(CHUNKS - 1)
    for k in range(CHUNKS):
        finish(k)
    for k in range(CHUNKS):
        for j in range(chips):
            to_core(k, j).wait_send()
            if j > 0:
                to_chip(k, j).wait_send()
        for t in range(1, depth):
            to_layer(k, t).wait_send()


def scatter(share, residual, chips, depth, collective_id):
    rows, width = residual.shape
    part = width // CHUNKS
    dma = pltpu.SemaphoreType.DMA
    vmem = pltpu.VMEM
    blocks = (CHUNKS, chips, depth, rows, part)
    return pl.pallas_call(
        functools.partial(scatter_kernel, chips, depth),
        out_shape=jax.ShapeDtypeStruct((rows, width), jnp.bfloat16),
        in_specs=[
            pl.BlockSpec(memory_space=pl.ANY),
            pl.BlockSpec(memory_space=pltpu.VMEM),
        ],
        out_specs=pl.BlockSpec(memory_space=pltpu.VMEM),
        scratch_shapes=[
            vmem(blocks, jnp.bfloat16),
            vmem(blocks, jnp.bfloat16),
            vmem(blocks, jnp.bfloat16),
            vmem((CHUNKS, depth, rows, part), jnp.bfloat16),
            vmem((CHUNKS, depth, rows, part), jnp.bfloat16),
            vmem((CHUNKS, rows, part), jnp.float32),
            dma((CHUNKS, chips)),
            dma((CHUNKS, chips)),
            dma((CHUNKS, chips)),
            dma((CHUNKS, chips)),
            dma((CHUNKS, chips)),
            dma((CHUNKS, depth)),
            dma((CHUNKS, depth)),
        ],
        compiler_params=pltpu.CompilerParams(
            collective_id=collective_id, has_side_effects=True, vmem_limit_bytes=56 * 1024 * 1024
        ),
    )(share.reshape(chips, 2, depth, rows, width), residual)


def attend(query, step_key_value, key_value_cache, lengths, owners):
    steps, row_dev, columns = query.shape
    heads_dev = columns // HEAD_SIZE
    cache_len = key_value_cache.shape[2]
    score_scale = HEAD_SIZE ** (-0.5)
    rows = query.reshape(steps, row_dev, heads_dev, HEAD_SIZE).transpose(1, 0, 2, 3)
    rows = rows.reshape(row_dev, steps * heads_dev, HEAD_SIZE)
    fresh = step_key_value.transpose(1, 2, 0, 3)
    usable = jnp.arange(cache_len, dtype=jnp.int32)[None, :] < lengths[:, None]
    cache_scores = (
        jnp.einsum("rhd,rjd->rhj", rows, key_value_cache[0], preferred_element_type=jnp.float32)
        * score_scale
    )
    cache_scores = jnp.where(usable[:, None, :], cache_scores, masked_score)
    fresh_scores = (
        jnp.einsum("rhd,rjd->rhj", rows, fresh[0], preferred_element_type=jnp.float32)
        * score_scale
    )
    step_of = jnp.arange(steps * heads_dev, dtype=jnp.int32) // heads_dev
    known = jnp.arange(steps, dtype=jnp.int32)[None, :] <= step_of[:, None]
    fresh_scores = jnp.where(known[None], fresh_scores, masked_score)
    top = jnp.maximum(
        jnp.max(cache_scores, axis=-1, keepdims=True), jnp.max(fresh_scores, axis=-1, keepdims=True)
    )
    cache_raised = jnp.exp(cache_scores - top)
    fresh_raised = jnp.exp(fresh_scores - top)
    total = jnp.sum(cache_raised, axis=-1, keepdims=True) + jnp.sum(
        fresh_raised, axis=-1, keepdims=True
    )
    cache_probs = (cache_raised / total).astype(jnp.bfloat16)
    fresh_probs = (fresh_raised / total).astype(jnp.bfloat16)
    attended = jnp.einsum(
        "rhj,rjd->rhd", cache_probs, key_value_cache[1], preferred_element_type=jnp.float32
    ) + jnp.einsum("rhj,rjd->rhd", fresh_probs, fresh[1], preferred_element_type=jnp.float32)
    attended = attended.astype(jnp.bfloat16).reshape(owners, row_dev // owners, steps, columns)
    return attended.transpose(0, 2, 1, 3).reshape(steps * row_dev, columns)


def per_device(
    query,
    step_key_value,
    key_value_cache,
    lengths,
    hidden_in,
    norm_gain,
    w_out,
    routes,
    gate_scores,
    expert_gate,
    expert_up,
    expert_down,
):
    ep_count = lax.axis_size("ep")
    tp_count = lax.axis_size("tp")
    chips = ep_count // 2
    steps, row_own = hidden_in.shape[:2]
    width = hidden_in.shape[2]
    cols = w_out.shape[1]
    expert_count = ep_count * tp_count * expert_gate.shape[0]

    weights = gate_scores / jnp.sum(gate_scores, axis=-1, keepdims=True)
    named = routes[..., None] == jnp.arange(expert_count, dtype=jnp.int32)
    dense = jnp.sum(jnp.where(named, weights[..., None], 0.0), axis=2)

    by_expert = dense.reshape(steps * row_own, expert_count).T[..., None]
    high = lax.reduce_precision(by_expert, 8, 7)
    middle = lax.reduce_precision(by_expert - high, 8, 7)
    pieces = jnp.concatenate([high, middle, by_expert - high - middle], axis=2)
    pieces = jnp.pad(pieces, ((0, 0), (0, 0), (0, 125))).astype(jnp.bfloat16)

    attended = attend(query, step_key_value, key_value_cache, lengths, tp_count)
    everyone = gather(attended, chips, 1, 1)
    partial_sums = jnp.dot(everyone, w_out, preferred_element_type=jnp.float32)
    partial_sums = partial_sums.astype(jnp.bfloat16).reshape(-1, steps * row_own, cols)
    outgoing = jnp.concatenate([partial_sums, pieces], axis=2)
    arrived = lax.all_to_all(outgoing, ("ep", "tp"), split_axis=0, concat_axis=0, tiled=True)
    my_weight = jnp.sum(arrived[..., cols : cols + 3].astype(jnp.float32), axis=2).reshape(-1, 1)
    arrived = arrived[..., :cols].reshape(ep_count, tp_count, steps * row_own, cols)
    projected = jnp.sum(arrived.astype(jnp.float32), axis=1).astype(jnp.bfloat16)
    row_major = projected.transpose(1, 0, 2).reshape(steps * row_own, width)
    own = hidden_in.reshape(steps * row_own, width)
    residual = own.astype(jnp.float32) + row_major.astype(jnp.float32)
    mean_square = jnp.mean(residual * residual, axis=-1, keepdims=True)
    normed = (residual * lax.rsqrt(mean_square + norm_eps) * norm_gain).astype(jnp.bfloat16)

    flat_rows = gather(normed, chips, tp_count, 2)
    gate_act = jnp.dot(flat_rows, expert_gate[0], preferred_element_type=jnp.float32)
    up_act = jnp.dot(flat_rows, expert_up[0], preferred_element_type=jnp.float32)
    hidden = (jax.nn.silu(gate_act) * up_act).astype(jnp.bfloat16)
    expert_out = jnp.dot(hidden, expert_down[0], preferred_element_type=jnp.float32).astype(
        jnp.bfloat16
    )
    share = (expert_out.astype(jnp.float32) * my_weight).astype(jnp.bfloat16)
    layer_out = scatter(share, residual, chips, tp_count, 3)
    return layer_out.reshape(steps, row_own, width)


def solution(mesh):
    placed = (
        P(None, "ep", "tp"),
        P(None, None, "ep", "tp"),
        P(None, "ep", None, "tp"),
        P("ep"),
        P(None, ("ep", "tp"), None),
        P(),
        P("tp", "ep"),
        P(None, ("ep", "tp"), None),
        P(None, ("ep", "tp"), None),
        P(("ep", "tp"), None, None),
        P(("ep", "tp"), None, None),
        P(("ep", "tp"), None, None),
    )
    return jax.shard_map(
        per_device,
        mesh=mesh,
        in_specs=placed,
        out_specs=P(None, ("ep", "tp"), None),
        check_vma=False,
    )
```
